32 devices in a mesh: row: 2 (over core), col: 4 (over y, x), depth: 4 (over z).
Axes of the slice: x: 2, y: 2, z: 4, core: 2. Of those that a mesh axis runs over, the one named last changes fastest.
Arguments:
- traces: bfloat16 [32768, 16384], P(('col', 'depth'), 'row'), may hold values from -0.03125 to 0.03125
- features: bfloat16 [32768, 2048], P(('col', 'depth'), 'row'), may hold values from -6 to 6
- next_features: bfloat16 [32768, 2048], P(('col', 'depth'), 'row'), may hold values from -6 to 6
Outputs:
- panels: float32 [16384, 2048], P('row', ('col', 'depth'))
The draws below stay inside these ranges and needn't reach their ends.
All inputs are finite; a program needn't handle non-finite values.
Results may differ from the reference program's by a relative error of at most 0.0028.
Values may be sent and summed in bfloat16 or wider, within the bound.
No kernel may reach another device: no remote copies, remote signals or barrier semaphores. Data moves between devices by JAX's collectives and lax.ppermute only.
A program may use at most 192 MiB of HBM per device.

```python
import jax
import jax.numpy as jnp
from jax import lax

F = 16384
PW = 1024
PANELS = 2
TOKENS = 32768


def spiked(entries, key, source, target, parts, factor):
    owner, partner = [(jnp.arange(entries.shape[position]) // (entries.shape[position] // parts)).reshape([-1 if axis == position else 1 for axis in range(entries.ndim)]) for position in (source, target)]
    chosen = jax.random.permutation(key, parts)[partner]
    strong = (owner == chosen) | (owner == (partner + parts // 2) % parts)
    return jnp.where(strong, factor * entries, entries)


def block_levels(key, shape, pieces, least, largest):
    level = 1.0
    for position, shards_of in pieces:
        heights = jax.random.uniform(jax.random.fold_in(jax.random.fold_in(key, 6), position), (shards_of,), jnp.float32, least / len(pieces), largest / len(pieces))
        level = level * jnp.repeat(jnp.exp(heights), shape[position] // shards_of).reshape((-1,) + (1,) * (len(shape) - 1 - position))
    return level


def normal_values(own_key, dims, spread, most, shards=(), held_as=jnp.bfloat16):
    array = jax.random.normal(own_key, dims, jnp.float32) * spread
    if len(shards) > 0:
        array = block_levels(own_key, dims, shards, -0.22, 0.18) * array
    return jnp.clip(array, min=-most, max=most).astype(held_as)


def heavy_noise(key, shape, scale, reach, pieces, heavy, held_as=jnp.bfloat16):
    result = scale * jax.random.normal(key, shape, jnp.float32)
    if pieces:
        result = result * block_levels(key, shape, pieces, -0.22, 0.18)
    return jnp.clip(spiked(result, jax.random.fold_in(key, 3), *heavy), -reach, reach).astype(held_as)


def setup_inputs(seed: int = 0) -> dict:
    seeds = jax.random.split(jax.random.key(seed), 4)
    return {
        "traces": normal_values(seeds[0], (TOKENS, F), TOKENS ** -0.5, 0.03125, ((0, 16), (1, 2))),
        "features": heavy_noise(seeds[1], (TOKENS, PANELS * PW), 1.0, 6.0, ((0, 16), (1, 2)), (0, 1, 16, 2.0)),
        "next_features": normal_values(seeds[2], (TOKENS, PANELS * PW), 1.0, 6.0, ((0, 16), (1, 2))),
    }


DISCOUNT = 0.99


def reference(traces, features, next_features):
    differences = (features.astype(jnp.float32) - DISCOUNT * next_features.astype(jnp.float32)).astype(jnp.bfloat16)
    differences = lax.optimization_barrier(differences).astype(jnp.float32)
    weights = traces.astype(jnp.float32)
    return lax.dot_general(weights, differences, (((0,), (0,)), ((), ())), precision=lax.Precision.HIGHEST, preferred_element_type=jnp.float32)
```

```python
import functools

import jax
import jax.numpy as jnp
from jax import lax
from jax.experimental import pallas as pl
from jax.experimental.pallas import tpu as pltpu
from jax.sharding import PartitionSpec as P

DISCOUNT = 0.99
LANES = 128
VMEM_LIMIT = 56 * 1024 * 1024
BRIEF = pl.CostEstimate(flops=0, bytes_accessed=0, transcendentals=0)

UNITS = (
    ("xlyh", 2),
    ("xlyh", 4),
    ("xlyh", 4),
    ("xlyh", 4),
    ("xlyh", 4),
    ("xlyh", 4),
    ("xlyh", 4),
    ("xlyh", 2),
    ("xlyh", 2),
    ("xlyh", 2),
)
ORDER = (
    0, 1, 2, 0, 3, 1, 0, 4, 2, 1, 5, 3, 0, 2, 6, 4, 1, 3, 0, 7, 5, 2, 4, 8,
    1, 9, 6, 5, 3, 7, 2, 4, 8, 6, 9, 3, 5, 7, 6, 7, 4, 8, 8, 9, 9, 5, 6, 7,
    8, 9,
)

MIRROR = {"x": "y", "y": "x", "l": "l", "h": "h"}


def half(x):
    return x.astype(jnp.bfloat16)


def full(x):
    return x.astype(jnp.float32)


def slot_of(order, bits):
    return bits[order[1]] * 4 + bits[order[2]] * 2 + bits[order[3]]


def product_kernel(orders, group, table, traces, own, other, after, *refs):
    keeps, sends, (held, sems) = refs[:2], refs[2:-2], refs[-2:]
    first = pl.program_id(0) == 0
    tall = traces.shape[1] // 2
    places = (3, 1, 2, 0)
    z_low, z_high = table[8] % 2, table[8] // 2

    def load(source, place):
        start = pl.multiple_of(table[2 * place + 1], group)
        return pltpu.make_async_copy(
            source.at[:, pl.ds(start, group)], held.at[place], sems.at[place]
        )

    @pl.when(first)
    def _():
        for place in places:

            @pl.when(table[2 * place] == 0)
            def _():
                load(own, place).start()

            @pl.when(table[2 * place] != 0)
            def _():
                load(other, place).start()

    def products(place):
        rows = traces[...]
        total = lax.dot_general(
            rows,
            held[place],
            (((0,), (0,)), ((), ())),
            preferred_element_type=jnp.float32,
        )
        pieces = [
            total[:, block * LANES : (block + 1) * LANES]
            for block in range(group // LANES)
        ]
        for chunk, order in enumerate(orders):
            mine = [p[chunk * tall : (chunk + 1) * tall] for p in pieces]
            if order[0] == "l":
                for high in range(len(mine) // 2):
                    bits = {
                        "x": place % 2,
                        "y": place // 2,
                        "h": lax.bitwise_xor(z_high, high),
                    }
                    slot = slot_of(order, bits)
                    even, odd = mine[2 * high], mine[2 * high + 1]
                    keeps[chunk][slot] = jnp.where(z_low == 0, even, odd)
                    sends[0][8 * chunk + slot] = half(jnp.where(z_low == 0, odd, even))
            else:
                for block, piece in enumerate(mine):
                    bits = {
                        "x": place % 2,
                        "y": place // 2,
                        "l": lax.bitwise_xor(z_low, block % 2),
                        "h": lax.bitwise_xor(z_high, block // 2),
                    }
                    slot = slot_of(order, bits)
                    if bits[order[0]]:
                        sends[chunk][slot] = half(piece)
                    else:
                        keeps[chunk][slot] = piece

    @pl.when(first)
    def _():
        for place in places:
            load(own, place).wait()
            products(place)

    @pl.when(jnp.logical_not(first))
    def _():
        for place in places:
            products(place)


def tall_of(first_row, height):
    return 256 if height % 256 == 0 and first_row % 512 == 0 else 128


def unit_products(orders, table, traces, own, other, first_row, height, after):
    tokens = traces.shape[0]
    tall = tall_of(first_row, height)
    group = own.shape[1] // 2
    first = first_row // (2 * tall)

    def block(slots):
        return pl.BlockSpec((slots, tall, LANES), lambda i, table: (0, i, 0))

    def shape(slots, dtype):
        return jax.ShapeDtypeStruct((slots, height, LANES), dtype)

    counts = [16] if orders[0][0] == "l" else [8, 8]
    outs = pl.pallas_call(
        functools.partial(product_kernel, orders, group),
        name="products",
        grid_spec=pltpu.PrefetchScalarGridSpec(
            num_scalar_prefetch=1,
            grid=(height // tall,),
            in_specs=[
                pl.BlockSpec((tokens, 2 * tall), lambda i, table: (0, first + i)),
                pl.BlockSpec(memory_space=pl.ANY),
                pl.BlockSpec(memory_space=pl.ANY),
                pl.BlockSpec(memory_space=pl.ANY),
            ],
            out_specs=[block(8), block(8)] + [block(count) for count in counts],
            scratch_shapes=[
                pltpu.VMEM((4, tokens, group), own.dtype),
                pltpu.SemaphoreType.DMA((4,)),
            ],
        ),
        out_shape=[shape(8, jnp.float32)] * 2
        + [shape(count, jnp.bfloat16) for count in counts],
        cost_estimate=BRIEF,
        compiler_params=pltpu.CompilerParams(vmem_limit_bytes=VMEM_LIMIT),
    )(table, traces, own, other, after)
    return outs[:2], outs[2:]


def sums_kernel(counts, *refs):
    terms, outs = refs[: sum(counts)], refs[sum(counts) + 1 :]
    totals = []
    for chunk in range(2):
        mine = terms[chunk * counts[0] : chunk * counts[0] + counts[chunk]]
        total = mine[0][...]
        for term in mine[1:]:
            total = total + full(term[...])
        totals.append(half(total))
    if len(outs) == 2:
        for out, total in zip(outs, totals):
            out[...] = total
    else:
        slots = totals[0].shape[0]
        outs[0][:slots] = totals[0]
        outs[0][slots:] = totals[1]


def unit_sums(slots, chunks, split, tall, after):
    height = chunks[0][0][0].shape[1]
    terms = chunks[0] + chunks[1]
    specs = [
        pl.BlockSpec((slots, tall, LANES), lambda i, place=start // slots + 1: (place, i, 0))
        for _, start in terms
    ]
    held = slots if split else 2 * slots
    shape = jax.ShapeDtypeStruct((held, height, LANES), jnp.bfloat16)
    block = pl.BlockSpec((held, tall, LANES), lambda i: (0, i, 0))
    return pl.pallas_call(
        functools.partial(sums_kernel, [len(c) for c in chunks]),
        name="sums",
        grid=(height // tall,),
        in_specs=specs + [pl.BlockSpec(memory_space=pl.ANY)],
        out_specs=[block] * (1 + split),
        out_shape=[shape] * (1 + split),
        cost_estimate=BRIEF,
        compiler_params=pltpu.CompilerParams(vmem_limit_bytes=VMEM_LIMIT),
    )(*[array for array, _ in terms], after)


def last_kernel(count, *refs):
    out, done = refs[-2:]
    tall = out.shape[0] // 2
    done[...] = jnp.zeros_like(done)
    for chunk in range(2):
        mine = refs[chunk * count : (chunk + 1) * count]
        total = mine[0][0]
        for term in mine[1:]:
            total = total + full(term[0])
        out[chunk * tall : (chunk + 1) * tall] = total


def unit_last(out, rows, chunks, first_row, tall, after):
    height = chunks[0][0][0].shape[1]
    first = first_row // (2 * tall)
    terms = chunks[0] + chunks[1]
    specs = [
        pl.BlockSpec((1, tall, LANES), lambda i, place=place: (place, i, 0))
        for _, place in terms
    ]
    operands = [array for array, _ in terms] + [after]
    aliases = {}
    if out is not None:
        aliases = {len(operands): 0}
        operands.append(out)
    return pl.pallas_call(
        functools.partial(last_kernel, len(chunks[0])),
        name="last",
        grid=(height // tall,),
        in_specs=specs + [pl.BlockSpec(memory_space=pl.ANY)] * (1 + len(aliases)),
        out_specs=[
            pl.BlockSpec((2 * tall, LANES), lambda i: (first + i, 0)),
            pl.BlockSpec((8, LANES), lambda i: (0, 0)),
        ],
        out_shape=[
            jax.ShapeDtypeStruct((rows, LANES), jnp.float32),
            jax.ShapeDtypeStruct((8, LANES), jnp.float32),
        ],
        input_output_aliases=aliases,
        cost_estimate=BRIEF,
        compiler_params=pltpu.CompilerParams(vmem_limit_bytes=VMEM_LIMIT),
    )(*operands)


def plan(rows):
    steps = rows // (2 * LANES)
    units, order = UNITS, ORDER
    if sum(share for _, share in units) != steps:
        units = (("xlyh", 1),) * steps
        order = [
            unit
            for turn in range(steps + 4)
            for unit in range(turn, turn - 5, -1)
            if 0 <= unit < steps
        ]
    starts, start = {}, 0
    for unit in sorted(range(len(units)), key=lambda u: units[u][1] % 2):
        starts[unit] = start
        start += units[unit][1] * 2 * LANES
    return [
        ((a, "".join(MIRROR[d] for d in a)), starts[unit], share * LANES)
        for unit, (a, share) in enumerate(units)
    ], order


def shards(sizes, traces, features, next_features):
    rows_n, cols_n, depth = sizes
    differences = half(full(features) - DISCOUNT * full(next_features))
    row, col, z = (lax.axis_index(name) for name in ("row", "col", "depth"))
    if rows_n == 2:
        own, flip = differences, row
        other = lax.ppermute(differences, "row", [(0, 1), (1, 0)])
    else:
        whole = lax.all_gather(differences, "row", axis=1, tiled=True)
        own, other = jnp.split(whole, 2, axis=1)
        flip = 0
    group = own.shape[1] // 2
    rows = traces.shape[1]

    entries = []
    for bits in range(4):
        near = lax.bitwise_xor(col, bits)
        entries += [lax.bitwise_xor(near // 2, flip), (near % 2) * group]
    table = jnp.stack(entries + [z]).astype(jnp.int32)

    def swap(v, dim):
        axis, size, bit = {
            "x": ("col", cols_n, 1),
            "y": ("col", cols_n, 2),
            "l": ("depth", depth, 1),
            "h": ("depth", depth, 2),
        }[dim]
        return lax.ppermute(v, axis, [(i, i ^ bit) for i in range(size)])

    units, order = plan(rows)
    terms = [None] * len(units)
    stages = [0] * len(units)
    after, out = table, None
    for unit in order:
        orders, first_row, height = units[unit]
        stage, tall = stages[unit], tall_of(first_row, height)
        stages[unit] += 1
        if stage == 4:
            out, after = unit_last(out, rows, terms[unit], first_row, tall, after)
            continue
        dims = [o[stage] for o in orders]
        slots = 8 >> stage
        if stage == 0:
            keeps, sends = unit_products(
                orders, table, traces, own, other, first_row, height, after
            )
            terms[unit] = [[(keep, 0)] for keep in keeps]
        else:
            sends = unit_sums(slots, terms[unit], dims[0] != dims[1], tall, after)
        after = sends[0]
        got = [swap(send, dim) for send, dim in zip(sends, dims)]
        for chunk in range(2):
            arrived = (got[chunk], 0) if len(got) == 2 else (got[0], slots * chunk)
            terms[unit][chunk].append(arrived)
    return out


def solution(mesh):
    sizes = tuple(mesh.shape[name] for name in ("row", "col", "depth"))
    spec = P(("col", "depth"), "row")
    return jax.shard_map(
        functools.partial(shards, sizes),
        mesh=mesh,
        in_specs=(spec, spec, spec),
        out_specs=P("row", ("col", "depth")),
        check_vma=False,
    )
```

```python
import functools

import jax
import jax.numpy as jnp
from jax import lax
from jax.experimental import pallas as pl
from jax.experimental.pallas import tpu as pltpu
from jax.sharding import PartitionSpec as P

DISCOUNT = 0.99
LANES = 128
VMEM_LIMIT = 56 * 1024 * 1024
LONG = pl.CostEstimate(flops=10**12, bytes_accessed=0, transcendentals=0)

UNITS = (
    ("flsh", 4),
    ("flsh", 4),
    ("flsh", 4),
    ("flsh", 4),
    ("flsh", 4),
    ("flsh", 4),
    ("flsh", 4),
    ("flsh", 4),
)
ORDER = (
    0, 1, 0, 2, 1, 0, 3, 2, 1, 0, 4, 3, 2, 1, 0, 5, 4, 3, 2, 1, 6, 5, 4, 3,
    2, 7, 6, 5, 4, 3, 7, 6, 5, 4, 7, 6, 5, 7, 6, 7,
)
STEP = 256


def half(x):
    return x.astype(jnp.bfloat16)


def full(x):
    return x.astype(jnp.float32)


def slot_of(order, bits):
    return bits[order[1]] * 4 + bits[order[2]] * 2 + bits[order[3]]


def product_kernel(order, table, traces, *refs):
    groups, keep, send, held, sems = refs[:4], *refs[5:]
    first = pl.program_id(0) == 0
    places = (1, 3, 0, 2)
    z_low, z_high = table[4] % 2, table[4] // 2

    def load(source, place):
        return pltpu.make_async_copy(source, held.at[place], sems.at[place])

    @pl.when(first)
    def _():
        for place in places:
            for index, source in enumerate(groups):

                @pl.when(table[place] == index)
                def _():
                    load(source, place).start()

    def products(place):
        total = lax.dot_general(
            traces[...],
            held[place],
            (((0,), (0,)), ((), ())),
            preferred_element_type=jnp.float32,
        )
        pieces = [
            total[:, block * LANES : (block + 1) * LANES]
            for block in range(held.shape[2] // LANES)
        ]
        bits = {"f": place % 2, "s": place // 2}
        if order[0] == "l":
            for high in range(len(pieces) // 2):
                bits["h"] = lax.bitwise_xor(z_high, high)
                slot = slot_of(order, bits)
                even, odd = pieces[2 * high], pieces[2 * high + 1]
                keep[slot] = jnp.where(z_low == 0, even, odd)
                send[slot] = half(jnp.where(z_low == 0, odd, even))
        else:
            for block, piece in enumerate(pieces):
                bits["l"] = lax.bitwise_xor(z_low, block % 2)
                bits["h"] = lax.bitwise_xor(z_high, block // 2)
                slot = slot_of(order, bits)
                if bits[order[0]]:
                    send[slot] = half(piece)
                else:
                    keep[slot] = piece

    @pl.when(first)
    def _():
        for place in places:
            load(groups[0], place).wait()
            products(place)

    @pl.when(jnp.logical_not(first))
    def _():
        for place in places:
            products(place)


def tall_of(first_row, height):
    return 2 * STEP if height % (2 * STEP) == 0 and first_row % (2 * STEP) == 0 else STEP


def unit_products(order, table, traces, groups, first_row, height, after):
    tokens = traces.shape[0]
    tall = tall_of(first_row, height)
    first = first_row // tall
    block = pl.BlockSpec((8, tall, LANES), lambda i, table: (0, i, 0))
    return pl.pallas_call(
        functools.partial(product_kernel, order),
        name="products",
        grid_spec=pltpu.PrefetchScalarGridSpec(
            num_scalar_prefetch=1,
            grid=(height // tall,),
            in_specs=[pl.BlockSpec((tokens, tall), lambda i, table: (0, first + i))]
            + [pl.BlockSpec(memory_space=pl.ANY)] * 5,
            out_specs=[block, block],
            scratch_shapes=[
                pltpu.VMEM((4,) + groups[0].shape, groups[0].dtype),
                pltpu.SemaphoreType.DMA((4,)),
            ],
        ),
        out_shape=[
            jax.ShapeDtypeStruct((8, height, LANES), jnp.float32),
            jax.ShapeDtypeStruct((8, height, LANES), jnp.bfloat16),
        ],
        cost_estimate=LONG,
        compiler_params=pltpu.CompilerParams(vmem_limit_bytes=VMEM_LIMIT),
    )(table, traces, *groups, after)


def total_of(terms):
    total = terms[0][...]
    for term in terms[1:]:
        total = total + full(term[...])
    return total


def sums_kernel(*refs):
    refs[-1][...] = half(total_of(refs[:-2]))


def unit_sums(slots, terms, tall, after):
    height = terms[0].shape[1]
    return pl.pallas_call(
        sums_kernel,
        name="sums",
        grid=(height // tall,),
        in_specs=[pl.BlockSpec((slots, tall, LANES), lambda i: (1, i, 0))] * len(terms)
        + [pl.BlockSpec(memory_space=pl.ANY)],
        out_specs=pl.BlockSpec((slots, tall, LANES), lambda i: (0, i, 0)),
        out_shape=jax.ShapeDtypeStruct((slots, height, LANES), jnp.bfloat16),
        cost_estimate=LONG,
        compiler_params=pltpu.CompilerParams(vmem_limit_bytes=VMEM_LIMIT),
    )(*terms, after)


def last_kernel(count, *refs):
    out, done = refs[-2:]
    out[...] = total_of(refs[:count])[0]
    done[...] = jnp.zeros_like(done)


def unit_last(out, rows, terms, first_row, tall, after):
    height = terms[0].shape[1]
    first = first_row // tall
    operands = list(terms) + [after]
    aliases = {}
    if out is not None:
        aliases = {len(operands): 0}
        operands.append(out)
    return pl.pallas_call(
        functools.partial(last_kernel, len(terms)),
        name="last",
        grid=(height // tall,),
        in_specs=[pl.BlockSpec((1, tall, LANES), lambda i: (0, i, 0))] * len(terms)
        + [pl.BlockSpec(memory_space=pl.ANY)] * (1 + len(aliases)),
        out_specs=[
            pl.BlockSpec((tall, LANES), lambda i: (first + i, 0)),
            pl.BlockSpec((8, LANES), lambda i: (0, 0)),
        ],
        out_shape=[
            jax.ShapeDtypeStruct((rows, LANES), jnp.float32),
            jax.ShapeDtypeStruct((8, LANES), jnp.float32),
        ],
        input_output_aliases=aliases,
        cost_estimate=LONG,
        compiler_params=pltpu.CompilerParams(vmem_limit_bytes=VMEM_LIMIT),
    )(*operands)


def plan(rows):
    steps = rows // STEP
    units, order = UNITS, ORDER
    if sum(share for _, share in units) != steps:
        units = (("flsh", 1),) * steps
        order = [
            unit
            for turn in range(steps + 4)
            for unit in range(turn, turn - 5, -1)
            if 0 <= unit < steps
        ]
    starts, start = {}, 0
    for unit in sorted(range(len(units)), key=lambda u: units[u][1] % 2):
        starts[unit] = start
        start += units[unit][1] * STEP
    return [
        (exchanges, starts[unit], share * STEP)
        for unit, (exchanges, share) in enumerate(units)
    ], order


def shards(sizes, traces, features, next_features):
    rows_n, cols_n, depth = sizes
    row, col, z = (lax.axis_index(name) for name in ("row", "col", "depth"))

    def differences(start, size):
        part = slice(start, start + size)
        return half(full(features[:, part]) - DISCOUNT * full(next_features[:, part]))

    if rows_n == 2:
        size = features.shape[1] // 2
        groups = [differences(0, size), differences(size, size)]
        groups += [lax.ppermute(g, "row", [(0, 1), (1, 0)]) for g in groups]
        flip = 2 * row
    else:
        mine = differences(0, features.shape[1])
        groups = jnp.split(lax.all_gather(mine, "row", axis=1, tiled=True), 4, axis=1)
        flip = 0
    rows = traces.shape[1]
    table = jnp.stack(
        [
            lax.bitwise_xor(lax.bitwise_xor(col, jnp.where(row % 2 == 0, even, odd)), flip)
            for even, odd in ((0, 0), (1, 2), (2, 1), (3, 3))
        ]
        + [z]
    ).astype(jnp.int32)

    def swap(v, dim):
        if dim in "lh":
            bit = 1 if dim == "l" else 2
            return lax.ppermute(v, "depth", [(i, i ^ bit) for i in range(depth)])
        pairs = [
            (r * cols_n + c, r * cols_n + (c ^ (1 if (dim == "f") == (r % 2 == 0) else 2)))
            for r in range(rows_n)
            for c in range(cols_n)
        ]
        return lax.ppermute(v, ("row", "col"), pairs)

    units, order = plan(rows)
    terms = [[] for _ in units]
    stages = [0] * len(units)
    after, out = table, None
    for unit in order:
        exchanges, first_row, height = units[unit]
        stage, tall = stages[unit], tall_of(first_row, height)
        stages[unit] += 1
        if stage == 4:
            out, after = unit_last(out, rows, terms[unit], first_row, tall, after)
            continue
        if stage == 0:
            keep, after = unit_products(
                exchanges, table, traces, groups, first_row, height, after
            )
            terms[unit].append(keep)
        else:
            after = unit_sums(8 >> stage, terms[unit], tall, after)
        terms[unit].append(swap(after, exchanges[stage]))
    return out


def solution(mesh):
    sizes = tuple(mesh.shape[name] for name in ("row", "col", "depth"))
    spec = P(("col", "depth"), "row")
    return jax.shard_map(
        functools.partial(shards, sizes),
        mesh=mesh,
        in_specs=(spec, spec, spec),
        out_specs=P("row", ("col", "depth")),
        check_vma=False,
    )
```

```python
import functools

import jax
import jax.numpy as jnp
from jax import lax
from jax.experimental import pallas as pl
from jax.experimental.pallas import tpu as pltpu
from jax.sharding import PartitionSpec as P

DISCOUNT = 0.99
LANES = 128
VMEM_LIMIT = 56 * 1024 * 1024
LONG = pl.CostEstimate(flops=10**12, bytes_accessed=0, transcendentals=0)

UNITS = (
    ("flsh", 2),
    ("flsh", 4),
    ("flsh", 4),
    ("flsh", 4),
    ("flsh", 4),
    ("flsh", 4),
    ("flsh", 4),
    ("flsh", 4),
    ("fslh", 2),
)
STEP = 256


def pipeline(count):
    order = []
    for turn in range(count + 4):
        order.append([turn] if turn < count else [])
        order.append([u for u in (turn - 1,) if 0 <= u < count])
        rest = [u for u in range(turn - 2, turn - 5, -1) if 0 <= u < count]
        split = len(rest) if turn < count or turn < 4 else len(rest) - 1
        order += [rest[:split], rest[split:]]
    return [group for group in order if group]


def half(x):
    return x.astype(jnp.bfloat16)


def full(x):
    return x.astype(jnp.float32)


def slot_of(order, bits):
    return bits[order[1]] * 4 + bits[order[2]] * 2 + bits[order[3]]


def product_kernel(order, table, traces, *refs):
    groups, keep, send, held, sems = refs[:4], *refs[5:]
    first = pl.program_id(0) == 0
    places = (1, 3, 0, 2)
    z_low, z_high = table[4] % 2, table[4] // 2

    def load(source, place):
        return pltpu.make_async_copy(source, held.at[place], sems.at[place])

    @pl.when(first)
    def _():
        for place in places:
            for index, source in enumerate(groups):

                @pl.when(table[place] == index)
                def _():
                    load(source, place).start()

    def products(place):
        total = lax.dot_general(
            traces[...],
            held[place],
            (((0,), (0,)), ((), ())),
            preferred_element_type=jnp.float32,
        )
        pieces = [
            total[:, block * LANES : (block + 1) * LANES]
            for block in range(held.shape[2] // LANES)
        ]
        bits = {"f": place % 2, "s": place // 2}
        if order[0] == "l":
            for high in range(len(pieces) // 2):
                bits["h"] = lax.bitwise_xor(z_high, high)
                slot = slot_of(order, bits)
                even, odd = pieces[2 * high], pieces[2 * high + 1]
                keep[slot] = jnp.where(z_low == 0, even, odd)
                send[slot] = half(jnp.where(z_low == 0, odd, even))
        else:
            for block, piece in enumerate(pieces):
                bits["l"] = lax.bitwise_xor(z_low, block % 2)
                bits["h"] = lax.bitwise_xor(z_high, block // 2)
                slot = slot_of(order, bits)
                if bits[order[0]]:
                    send[slot] = half(piece)
                else:
                    keep[slot] = piece

    @pl.when(first)
    def _():
        for place in places:
            load(groups[0], place).wait()
            products(place)

    @pl.when(jnp.logical_not(first))
    def _():
        for place in places:
            products(place)


def tall_of(first_row, height):
    return 2 * STEP if height % (2 * STEP) == 0 and first_row % (2 * STEP) == 0 else STEP


def unit_products(order, table, traces, groups, first_row, height, after):
    tokens = traces.shape[0]
    tall = tall_of(first_row, height)
    first = first_row // tall
    block = pl.BlockSpec((8, tall, LANES), lambda i, table: (0, i, 0))
    return pl.pallas_call(
        functools.partial(product_kernel, order),
        name="products",
        grid_spec=pltpu.PrefetchScalarGridSpec(
            num_scalar_prefetch=1,
            grid=(height // tall,),
            in_specs=[pl.BlockSpec((tokens, tall), lambda i, table: (0, first + i))]
            + [pl.BlockSpec(memory_space=pl.ANY)] * 5,
            out_specs=[block, block],
            scratch_shapes=[
                pltpu.VMEM((4,) + groups[0].shape, groups[0].dtype),
                pltpu.SemaphoreType.DMA((4,)),
            ],
        ),
        out_shape=[
            jax.ShapeDtypeStruct((8, height, LANES), jnp.float32),
            jax.ShapeDtypeStruct((8, height, LANES), jnp.bfloat16),
        ],
        cost_estimate=LONG,
        compiler_params=pltpu.CompilerParams(vmem_limit_bytes=VMEM_LIMIT),
    )(table, traces, *groups, after)


def total_of(terms):
    total = terms[0][...]
    for term in terms[1:]:
        total = total + full(term[...])
    return total


def sums_kernel(counts, stages, *refs):
    outs = refs[len(refs) - len(stages) - (4 in stages) :]
    start = 0
    for count, stage, out in zip(counts, stages, outs):
        total = total_of(refs[start : start + count])
        out[...] = total[0] if stage == 4 else half(total)
        start += count
    if 4 in stages:
        outs[-1][...] = jnp.zeros_like(outs[-1])


def unit_sums(parts, out, rows, after):
    steps = 2
    operands, in_specs, out_specs, out_shape, aliases = [], [], [], [], {}
    for terms, stage, first_row in parts:
        height = terms[0].shape[1]
        tall = height // steps
        slots = max(8 >> stage, 1)
        if stage == 4:
            place, first = 0, first_row // tall
            out_specs.append(pl.BlockSpec((tall, LANES), lambda i, first=first: (first + i, 0)))
            out_specs.append(pl.BlockSpec((8, LANES), lambda i: (0, 0)))
            out_shape.append(jax.ShapeDtypeStruct((rows, LANES), jnp.float32))
            out_shape.append(jax.ShapeDtypeStruct((8, LANES), jnp.float32))
        else:
            place = 1
            out_specs.append(pl.BlockSpec((slots, tall, LANES), lambda i: (0, i, 0)))
            out_shape.append(jax.ShapeDtypeStruct((slots, height, LANES), jnp.bfloat16))
        in_specs += [
            pl.BlockSpec((slots, tall, LANES), lambda i, place=place: (place, i, 0))
        ] * len(terms)
        operands += terms
    operands.append(after)
    stages = [stage for _, stage, _ in parts]
    if 4 in stages and out is not None:
        aliases = {len(operands): len(parts) - 1}
        operands.append(out)
    in_specs += [pl.BlockSpec(memory_space=pl.ANY)] * (1 + len(aliases))
    return pl.pallas_call(
        functools.partial(sums_kernel, [len(terms) for terms, _, _ in parts], stages),
        name="sums",
        grid=(steps,),
        in_specs=in_specs,
        out_specs=out_specs,
        out_shape=out_shape,
        input_output_aliases=aliases,
        cost_estimate=LONG,
        compiler_params=pltpu.CompilerParams(vmem_limit_bytes=VMEM_LIMIT),
    )(*operands)


def plan(rows):
    steps = rows // STEP
    units = UNITS
    if sum(share for _, share in units) != steps:
        units = (("flsh", 1),) * steps
    starts, start = {}, 0
    for unit in sorted(range(len(units)), key=lambda u: -units[u][1]):
        starts[unit] = start
        start += units[unit][1] * STEP
    return [
        (exchanges, starts[unit], share * STEP)
        for unit, (exchanges, share) in enumerate(units)
    ], pipeline(len(units))


def shards(sizes, traces, features, next_features):
    rows_n, cols_n, depth = sizes
    row, col, z = (lax.axis_index(name) for name in ("row", "col", "depth"))

    def differences(start, size):
        part = slice(start, start + size)
        return half(full(features[:, part]) - DISCOUNT * full(next_features[:, part]))

    if rows_n == 2:
        size = features.shape[1] // 2
        groups = [differences(0, size), differences(size, size)]
        groups += [lax.ppermute(g, "row", [(0, 1), (1, 0)]) for g in groups]
        flip = 2 * row
    else:
        mine = differences(0, features.shape[1])
        groups = jnp.split(lax.all_gather(mine, "row", axis=1, tiled=True), 4, axis=1)
        flip = 0
    rows = traces.shape[1]
    table = jnp.stack(
        [
            lax.bitwise_xor(lax.bitwise_xor(col, jnp.where(row % 2 == 0, even, odd)), flip)
            for even, odd in ((0, 0), (1, 2), (2, 1), (3, 3))
        ]
        + [z]
    ).astype(jnp.int32)

    def swap(v, dim):
        if dim in "lh":
            bit = 1 if dim == "l" else 2
            return lax.ppermute(v, "depth", [(i, i ^ bit) for i in range(depth)])
        pairs = [
            (r * cols_n + c, r * cols_n + (c ^ (1 if (dim == "f") == (r % 2 == 0) else 2)))
            for r in range(rows_n)
            for c in range(cols_n)
        ]
        return lax.ppermute(v, ("row", "col"), pairs)

    units, order = plan(rows)
    terms = [[] for _ in units]
    stages = [0] * len(units)
    after, out = table, None
    for group in order:
        parts = []
        for unit in group:
            exchanges, first_row, height = units[unit]
            if stages[unit] == 0:
                keep, after = unit_products(
                    exchanges, table, traces, groups, first_row, height, after
                )
                terms[unit] += [keep, swap(after, exchanges[0])]
            else:
                parts.append((terms[unit], stages[unit], first_row))
        if parts:
            sums = unit_sums(parts, out, rows, after)
            after = sums[-1]
            if parts[-1][1] == 4:
                out = sums[-2]
            for unit, got in zip(group, sums):
                if stages[unit] < 4:
                    terms[unit].append(swap(got, units[unit][0][stages[unit]]))
        for unit in group:
            stages[unit] += 1
    return out


def solution(mesh):
    sizes = tuple(mesh.shape[name] for name in ("row", "col", "depth"))
    spec = P(("col", "depth"), "row")
    return jax.shard_map(
        functools.partial(shards, sizes),
        mesh=mesh,
        in_specs=(spec, spec, spec),
        out_specs=P("row", ("col", "depth")),
        check_vma=False,
    )
```

```python
import functools

import jax
import jax.numpy as jnp
from jax import lax
from jax.experimental import pallas as pl
from jax.experimental.pallas import tpu as pltpu
from jax.sharding import PartitionSpec as P

DISCOUNT = 0.99
LANES = 128
VMEM_LIMIT = 56 * 1024 * 1024
LONG = pl.CostEstimate(flops=10**12, bytes_accessed=0, transcendentals=0)

UNITS = (
    ("flsh", 4),
    ("flsh", 4),
    ("flsh", 4),
    ("flsh", 4),
    ("flsh", 4),
    ("flsh", 4),
    ("flsh", 4),
    ("flsh", 2),
    ("fslh", 2),
)
STEP = 256


def pipeline(count):
    order = []
    for turn in range(count + 4):
        order.append([turn] if turn < count or turn < 4 else [])
        order.append([u for u in (turn - 1,) if 0 <= u < count])
        rest = [u for u in range(turn - 2, turn - 5, -1) if 0 <= u < count]
        split = len(rest) if turn < count or turn < 4 else len(rest) - 1
        order += [rest[:split], rest[split:]]
    return [group for group in order if group]


def half(x):
    return x.astype(jnp.bfloat16)


def full(x):
    return x.astype(jnp.float32)


def slot_of(order, bits):
    return bits[order[1]] * 4 + bits[order[2]] * 2 + bits[order[3]]


def product_kernel(order, table, traces, *refs):
    groups, keep, send, held, sems = refs[:4], *refs[5:]
    first = pl.program_id(0) == 0
    places = (1, 3, 0, 2)
    z_low, z_high = table[4] % 2, table[4] // 2

    def load(source, place):
        return pltpu.make_async_copy(source, held.at[place], sems.at[place])

    @pl.when(first)
    def _():
        for place in places:
            for index, source in enumerate(groups):

                @pl.when(table[place] == index)
                def _():
                    load(source, place).start()

    def products(place):
        total = lax.dot_general(
            traces[...],
            held[place],
            (((0,), (0,)), ((), ())),
            preferred_element_type=jnp.float32,
        )
        pieces = [
            total[:, block * LANES : (block + 1) * LANES]
            for block in range(held.shape[2] // LANES)
        ]
        bits = {"f": place % 2, "s": place // 2}
        if order[0] == "l":
            for high in range(len(pieces) // 2):
                bits["h"] = lax.bitwise_xor(z_high, high)
                slot = slot_of(order, bits)
                even, odd = pieces[2 * high], pieces[2 * high + 1]
                keep[slot] = jnp.where(z_low == 0, even, odd)
                send[slot] = half(jnp.where(z_low == 0, odd, even))
        else:
            for block, piece in enumerate(pieces):
                bits["l"] = lax.bitwise_xor(z_low, block % 2)
                bits["h"] = lax.bitwise_xor(z_high, block // 2)
                slot = slot_of(order, bits)
                if bits[order[0]]:
                    send[slot] = half(piece)
                else:
                    keep[slot] = piece

    @pl.when(first)
    def _():
        for place in places:
            load(groups[0], place).wait()
            products(place)

    @pl.when(jnp.logical_not(first))
    def _():
        for place in places:
            products(place)


def tall_of(first_row, height):
    return 2 * STEP if height % (2 * STEP) == 0 and first_row % (2 * STEP) == 0 else STEP


def unit_products(order, table, traces, groups, first_row, height, after):
    tokens = traces.shape[0]
    tall = tall_of(first_row, height)
    first = first_row // tall
    block = pl.BlockSpec((8, tall, LANES), lambda i, table: (0, i, 0))
    return pl.pallas_call(
        functools.partial(product_kernel, order),
        name="products",
        grid_spec=pltpu.PrefetchScalarGridSpec(
            num_scalar_prefetch=1,
            grid=(height // tall,),
            in_specs=[pl.BlockSpec((tokens, tall), lambda i, table: (0, first + i))]
            + [pl.BlockSpec(memory_space=pl.ANY)] * 5,
            out_specs=[block, block],
            scratch_shapes=[
                pltpu.VMEM((4,) + groups[0].shape, groups[0].dtype),
                pltpu.SemaphoreType.DMA((4,)),
            ],
        ),
        out_shape=[
            jax.ShapeDtypeStruct((8, height, LANES), jnp.float32),
            jax.ShapeDtypeStruct((8, height, LANES), jnp.bfloat16),
        ],
        cost_estimate=LONG,
        compiler_params=pltpu.CompilerParams(vmem_limit_bytes=VMEM_LIMIT),
    )(table, traces, *groups, after)


def total_of(terms):
    total = terms[0][...]
    for term in terms[1:]:
        total = total + full(term[...])
    return total


def sums_kernel(counts, stages, *refs):
    outs = refs[len(refs) - len(stages) - (4 in stages) :]
    start = 0
    for count, stage, out in zip(counts, stages, outs):
        total = total_of(refs[start : start + count])
        out[...] = total[0] if stage == 4 else half(total)
        start += count
    if 4 in stages:
        outs[-1][...] = jnp.zeros_like(outs[-1])


def unit_sums(parts, out, rows, after):
    steps = 2
    operands, in_specs, out_specs, out_shape, aliases = [], [], [], [], {}
    for terms, stage, first_row in parts:
        height = terms[0].shape[1]
        tall = height // steps
        slots = max(8 >> stage, 1)
        if stage == 4:
            place, first = 0, first_row // tall
            out_specs.append(pl.BlockSpec((tall, LANES), lambda i, first=first: (first + i, 0)))
            out_specs.append(pl.BlockSpec((8, LANES), lambda i: (0, 0)))
            out_shape.append(jax.ShapeDtypeStruct((rows, LANES), jnp.float32))
            out_shape.append(jax.ShapeDtypeStruct((8, LANES), jnp.float32))
        else:
            place = 1
            out_specs.append(pl.BlockSpec((slots, tall, LANES), lambda i: (0, i, 0)))
            out_shape.append(jax.ShapeDtypeStruct((slots, height, LANES), jnp.bfloat16))
        in_specs += [
            pl.BlockSpec((slots, tall, LANES), lambda i, place=place: (place, i, 0))
        ] * len(terms)
        operands += terms
    operands.append(after)
    stages = [stage for _, stage, _ in parts]
    if 4 in stages and out is not None:
        aliases = {len(operands): len(parts) - 1}
        operands.append(out)
    in_specs += [pl.BlockSpec(memory_space=pl.ANY)] * (1 + len(aliases))
    return pl.pallas_call(
        functools.partial(sums_kernel, [len(terms) for terms, _, _ in parts], stages),
        name="sums",
        grid=(steps,),
        in_specs=in_specs,
        out_specs=out_specs,
        out_shape=out_shape,
        input_output_aliases=aliases,
        cost_estimate=LONG,
        compiler_params=pltpu.CompilerParams(vmem_limit_bytes=VMEM_LIMIT),
    )(*operands)


def plan(rows):
    steps = rows // STEP
    units = UNITS
    if sum(share for _, share in units) != steps:
        units = (("flsh", 1),) * steps
    starts, start = {}, 0
    for unit in sorted(range(len(units)), key=lambda u: -units[u][1]):
        starts[unit] = start
        start += units[unit][1] * STEP
    return [
        (exchanges, starts[unit], share * STEP)
        for unit, (exchanges, share) in enumerate(units)
    ], pipeline(len(units))


def shards(sizes, traces, features, next_features):
    rows_n, cols_n, depth = sizes
    row, col, z = (lax.axis_index(name) for name in ("row", "col", "depth"))

    def differences(start, size):
        part = slice(start, start + size)
        return half(full(features[:, part]) - DISCOUNT * full(next_features[:, part]))

    if rows_n == 2:
        size = features.shape[1] // 2
        groups = [differences(0, size), differences(size, size)]
        groups += [lax.ppermute(g, "row", [(0, 1), (1, 0)]) for g in groups]
        flip = 2 * row
    else:
        mine = differences(0, features.shape[1])
        groups = jnp.split(lax.all_gather(mine, "row", axis=1, tiled=True), 4, axis=1)
        flip = 0
    rows = traces.shape[1]
    table = jnp.stack(
        [
            lax.bitwise_xor(lax.bitwise_xor(col, jnp.where(row % 2 == 0, even, odd)), flip)
            for even, odd in ((0, 0), (1, 2), (2, 1), (3, 3))
        ]
        + [z]
    ).astype(jnp.int32)

    def swap(v, dim):
        if dim in "lh":
            bit = 1 if dim == "l" else 2
            return lax.ppermute(v, "depth", [(i, i ^ bit) for i in range(depth)])
        pairs = [
            (r * cols_n + c, r * cols_n + (c ^ (1 if (dim == "f") == (r % 2 == 0) else 2)))
            for r in range(rows_n)
            for c in range(cols_n)
        ]
        return lax.ppermute(v, ("row", "col"), pairs)

    units, order = plan(rows)
    terms = [[] for _ in units]
    stages = [0] * len(units)
    after, out = table, None
    for group in order:
        parts = []
        for unit in group:
            exchanges, first_row, height = units[unit]
            if stages[unit] == 0:
                keep, after = unit_products(
                    exchanges, table, traces, groups, first_row, height, after
                )
                terms[unit] += [keep, swap(after, exchanges[0])]
            else:
                parts.append((terms[unit], stages[unit], first_row))
        if parts:
            sums = unit_sums(parts, out, rows, after)
            after = sums[-1]
            if parts[-1][1] == 4:
                out = sums[-2]
            for unit, got in zip(group, sums):
                if stages[unit] < 4:
                    terms[unit].append(swap(got, units[unit][0][stages[unit]]))
        for unit in group:
            stages[unit] += 1
    return out


def solution(mesh):
    sizes = tuple(mesh.shape[name] for name in ("row", "col", "depth"))
    spec = P(("col", "depth"), "row")
    return jax.shard_map(
        functools.partial(shards, sizes),
        mesh=mesh,
        in_specs=(spec, spec, spec),
        out_specs=P("row", ("col", "depth")),
        check_vma=False,
    )
```
